128 devices in a mesh: dp: 32 (over z, x, core), mp: 4 (over y).
Axes of the slice: x: 4, y: 4, z: 4, core: 2. Of those that a mesh axis runs over, the one named last changes fastest.
Arguments:
- patch_rows: bfloat16 [32768, 1664], P(('dp', 'mp')), may hold values from -64 to 64
- packing: int32 [2, 32768], P(None, ('dp', 'mp')), may hold values from 0 to 255, as said below
- segment: int32 [32768], P('dp'), may hold values from 0 to 48, as said below
- coords: int32 [2, 32768], P(None, ('dp', 'mp')), may hold values from 0 to 15, as said below
- pos_rows: bfloat16 [16, 1664], replicated, may hold values from -3 to 3
- pos_cols: bfloat16 [16, 1664], replicated, may hold values from -3 to 3
- norm_gain: bfloat16 [1664], replicated, may hold values from 0.25 to 1.75
- w_qkv: bfloat16 [1664, 3, 1664], P(None, None, 'mp'), may hold values from -1.25 to 1.25
- w_out: bfloat16 [1664, 1664], P('mp'), may hold values from -0.4375 to 0.4375
- cotangent: bfloat16 [32768, 1664], P(('dp', 'mp')), may hold values from -6 to 6
Outputs:
- output: bfloat16 [32768, 1664], P(('dp', 'mp'))
- d_patches: bfloat16 [32768, 1664], P(('dp', 'mp'))
- grad_qkv: float32 [1664, 3, 1664], P(None, None, 'mp')
- grad_out: float32 [1664, 1664], P('mp')
The draws below stay inside these ranges and needn't reach their ends.
Inputs may be any that keep to these rules, and one draw needn't show every extreme that they name: `packing`: each loader row goes to a device of the same mp index; every row of every device receives exactly one loader row. From one device to one device at most 16 rows go, and every device sends exactly 16 rows to one device. The counts from a device to the devices of its mp index form the same list on every device, in an order that differs from device to device. `segment`: within each packed sequence the image numbers start at 0 and rise by one from image to image; an image holds at most 256 patches, the first image of every sequence exactly that many, and every image but a sequence's last has at least 4 patch rows and columns. Some sequence holds as many images as fit. `coords`: patches of an image fill its grid row by row; the last image of a sequence may be cut short.
All inputs are finite; a program needn't handle non-finite values.
Results may differ from the reference program's by a relative error of at most 0.034.
Values may be sent and summed in bfloat16 or wider, within the bound.
A program may use at most 128 MiB of HBM per device.

```python
import jax
import jax.numpy as jnp
from jax import lax

D = 1664
HEADS = 16
HD = 104
ROWS_DEV = 256
GRID = 16
SEQ = 1024
TOTAL = 32768
N_DP = 32
N_MP = 4


def image_layout(key):
    least_side = max(1, GRID // 4)
    most_images = SEQ // (least_side * least_side)
    width_key, height_key = jax.random.split(key)
    widths = jax.random.randint(width_key, (N_DP, most_images), least_side, GRID + 1)
    heights = jax.random.randint(height_key, (N_DP, most_images), least_side, GRID + 1)
    first_image = (jnp.arange(most_images) == 0)[None, :]
    fullest = (jnp.arange(N_DP) == 0)[:, None]
    widths = jnp.where(fullest, least_side, widths)
    heights = jnp.where(fullest, least_side, heights)
    widths = jnp.where(first_image, GRID, widths)
    heights = jnp.where(first_image, GRID, heights)
    lengths = widths * heights
    image_ends = jnp.cumsum(lengths, axis=1)
    image_starts = image_ends - lengths
    places = jnp.arange(SEQ)
    segment = jnp.sum((image_ends[:, None, :] <= places[None, :, None]).astype(jnp.int32), axis=-1)
    offset = places[None, :] - jnp.take_along_axis(image_starts, segment, axis=1)
    row_width = jnp.take_along_axis(widths, segment, axis=1)
    return (segment.astype(jnp.int32), (offset // row_width).astype(jnp.int32), (offset % row_width).astype(jnp.int32))


def draw_segment(key, part):
    segment, grid_row, grid_col = image_layout(key)
    return segment.reshape(TOTAL).astype(jnp.int32)


def draw_coords(key, part):
    segment, grid_row, grid_col = image_layout(key)
    return jnp.stack([grid_row.reshape(TOTAL), grid_col.reshape(TOTAL)]).astype(jnp.int32)


def lane_routes(lane_key):
    mean_count = ROWS_DEV // N_DP
    size_key, dest_key, place_key, recv_key, send_key = jax.random.split(lane_key, 5)
    jitter = jax.random.randint(size_key, (N_DP - 2,), 0, mean_count)
    counts = jnp.concatenate([jnp.array([2 * mean_count, 0], jnp.int32), (mean_count + jitter - jnp.roll(jitter, 1)).astype(jnp.int32)])
    count_ends = jnp.cumsum(counts)
    places = jnp.arange(ROWS_DEV)
    labels = jnp.sum((count_ends[None, :] <= places[:, None]).astype(jnp.int32), axis=1)
    dest_order = jax.random.permutation(dest_key, N_DP)
    source_place = jax.random.permutation(place_key, N_DP)
    dest_group = dest_order[(source_place[:, None] + labels[None, :]) % N_DP]
    recv_perm = jax.vmap(lambda sub_key: jax.random.permutation(sub_key, ROWS_DEV))(jax.random.split(recv_key, N_DP))
    dest_slot = recv_perm[dest_group, places[None, :]]
    send_perm = jax.vmap(lambda sub_key: jax.random.permutation(sub_key, ROWS_DEV))(jax.random.split(send_key, N_DP))
    sources = jnp.arange(N_DP)[:, None]
    out_group = jnp.zeros((N_DP, ROWS_DEV), jnp.int32).at[sources, send_perm].set(dest_group)
    out_slot = jnp.zeros((N_DP, ROWS_DEV), jnp.int32).at[sources, send_perm].set(dest_slot)
    return (out_group, out_slot)


def draw_packing(key, part):
    key = jax.random.fold_in(key, 11)
    groups, slots = jax.vmap(lane_routes)(jax.random.split(key, N_MP))
    groups = jnp.transpose(groups, (1, 0, 2)).reshape(TOTAL)
    slots = jnp.transpose(slots, (1, 0, 2)).reshape(TOTAL)
    return jnp.stack([groups, slots]).astype(jnp.int32)


def draw_patch_rows(key, part):
    key = jax.random.fold_in(key, 21)
    base_key, row_key, col_key = jax.random.split(key, 3)
    col_scale = jnp.exp(jax.random.uniform(col_key, (1, D), jnp.float32, jnp.log(0.3), jnp.log(3.0)))
    values = jax.random.normal(base_key, (TOTAL, D), jnp.float32)
    row_scale = jnp.exp(jax.random.uniform(row_key, (TOTAL, 1), jnp.float32, jnp.log(0.3), jnp.log(3.0)))
    values = values * row_scale * col_scale
    return jnp.clip(values, -64.0, 64.0).astype(jnp.bfloat16)


def draw_w_qkv(key, part):
    key = jax.random.fold_in(key, 31)
    base_key = jax.random.fold_in(key, 0)
    values = jax.random.normal(base_key, (D, 3, HEADS * HD), jnp.float32) * D ** (-0.5)
    return jnp.clip(values, -1.25, 1.25).astype(jnp.bfloat16)


def steps_of(stream_key, dims, cuts, smallest, high):
    level, own = 1.0, jax.random.fold_in(stream_key, 6)
    for position, blocks in cuts:
        steps = jnp.exp(jax.random.uniform(jax.random.fold_in(own, position), (blocks,), jnp.float32, smallest / len(cuts), high / len(cuts)))
        level = level * jnp.repeat(steps, dims[position] // blocks).reshape([-1 if axis == position else 1 for axis in range(len(dims))])
    return level


def noise(rng, dims, width, bound, pieces=(), held_as=jnp.bfloat16):
    drawn = jax.random.normal(rng, dims, jnp.float32) * width
    if len(pieces) > 0:
        drawn = steps_of(rng, dims, pieces, -0.22, 0.18) * drawn
    return jnp.clip(drawn, min=-bound, max=bound).astype(held_as)


def setup_inputs(seed: int = 0) -> dict:
    key_of = jax.random.split(jax.random.key(seed), 11)
    patch_rows = draw_patch_rows(jax.random.fold_in(key_of[10], 71), 0)
    packing = draw_packing(jax.random.fold_in(key_of[10], 71), 0)
    segment = draw_segment(jax.random.fold_in(key_of[10], 71), 0)
    coords = draw_coords(jax.random.fold_in(key_of[10], 71), 0)
    pos_rows = noise(key_of[4], (GRID, D), 0.5, 3.0)
    pos_cols = noise(key_of[5], (GRID, D), 0.5, 3.0)
    norm_gain = jnp.clip(1.0 + 0.15 * jax.random.normal(key_of[6], (D,), jnp.float32), 0.25, 1.75).astype(jnp.bfloat16)
    w_qkv = draw_w_qkv(jax.random.fold_in(key_of[10], 71), 0)
    w_out = noise(key_of[8], (HEADS * HD, D), (2 * HD) ** -0.5, 0.4375, ((0, 4),))
    cotangent = noise(key_of[9], (TOTAL, D), 1.0, 6.0, ((0, 128),))
    return dict(patch_rows=patch_rows, packing=packing, segment=segment, coords=coords, pos_rows=pos_rows, pos_cols=pos_cols, norm_gain=norm_gain, w_qkv=w_qkv, w_out=w_out, cotangent=cotangent)


def layer_norm(values):
    row_mean = lax.optimization_barrier(jnp.mean(values, axis=-1, keepdims=True))
    centered = values - row_mean
    variance = lax.optimization_barrier(jnp.mean(centered * centered, axis=-1, keepdims=True))
    inv_std = lax.rsqrt(variance + 1e-06)
    return (centered * inv_std, inv_std)

def reference(patch_rows, packing, segment, coords, pos_rows, pos_cols, norm_gain, w_qkv, w_out, cotangent):
    group_width = HEADS * HD // N_MP
    row_index = jnp.arange(TOTAL, dtype=jnp.int32)
    lane_index = row_index // ROWS_DEV % N_MP
    target = ((packing[0] * N_MP + lane_index) * ROWS_DEV + packing[1]).astype(jnp.int32)
    packed = jnp.zeros((TOTAL, D), jnp.bfloat16).at[target].set(patch_rows)
    stream = (packed.astype(jnp.float32) + jnp.take(pos_rows, coords[0], axis=0).astype(jnp.float32) + jnp.take(pos_cols, coords[1], axis=0).astype(jnp.float32)).astype(jnp.bfloat16)
    score_scale = HD ** (-0.5)
    gain_f = norm_gain.astype(jnp.float32)
    w_flat = w_qkv.reshape(D, 3 * HEADS * HD)
    w_groups = w_qkv.reshape(D, 3, N_MP, group_width).astype(jnp.float32)
    out_groups = w_out.reshape(N_MP, group_width, D).astype(jnp.float32)

    def slot_step(totals, inputs):
        qkv_total, out_total = totals
        stream_s, segment_s, cot_s = inputs
        stream_f = stream_s.astype(jnp.float32)
        unit, inv_std = layer_norm(stream_f)
        normed = (unit * gain_f).astype(jnp.bfloat16)
        qkv = jnp.dot(normed, w_flat, preferred_element_type=jnp.float32).astype(jnp.bfloat16)
        qkv = qkv.reshape(SEQ, 3, HEADS, HD)
        query = qkv[:, 0].astype(jnp.float32)
        keys = qkv[:, 1].astype(jnp.float32)
        values = qkv[:, 2].astype(jnp.float32)
        same_image = segment_s[:, None] == segment_s[None, :]
        scores = jnp.einsum('qhd,khd->hqk', query, keys) * score_scale
        scores = jnp.where(same_image[None], scores, -1e+30)
        row_max = lax.optimization_barrier(jnp.max(scores, axis=-1, keepdims=True))
        expo = jnp.where(same_image[None], jnp.exp(scores - row_max), 0.0)
        prob = expo / lax.optimization_barrier(jnp.sum(expo, axis=-1, keepdims=True))
        prob_b = prob.astype(jnp.bfloat16)
        attended = jnp.einsum('hqk,khd->qhd', prob_b.astype(jnp.float32), values).astype(jnp.bfloat16)
        attended_f = attended.reshape(SEQ, N_MP, group_width).astype(jnp.float32)
        parts = jnp.einsum('sgh,ghd->gsd', attended_f, out_groups)
        parts = lax.optimization_barrier(parts.astype(jnp.bfloat16)).astype(jnp.float32)
        output_s = (stream_f + lax.optimization_barrier(jnp.sum(parts, axis=0))).astype(jnp.bfloat16)
        attended_flat = attended.reshape(SEQ, HEADS * HD)
        out_grad = jnp.dot(attended_flat.T, cot_s, preferred_element_type=jnp.float32)
        d_attended = jnp.dot(cot_s, w_out.T, preferred_element_type=jnp.float32).astype(jnp.bfloat16)
        d_att_f = d_attended.reshape(SEQ, HEADS, HD).astype(jnp.float32)
        att_f = attended.astype(jnp.float32)
        delta = jnp.einsum('qhd,qhd->hq', d_att_f, att_f)
        d_prob = jnp.einsum('qhd,khd->hqk', d_att_f, values)
        d_score = (prob * (d_prob - delta[:, :, None]) * score_scale).astype(jnp.bfloat16)
        d_score_f = d_score.astype(jnp.float32)
        d_query = jnp.einsum('hqk,khd->qhd', d_score_f, keys).astype(jnp.bfloat16)
        d_key = jnp.einsum('hqk,qhd->khd', d_score_f, query).astype(jnp.bfloat16)
        d_value = jnp.einsum('hqk,qhd->khd', prob_b.astype(jnp.float32), d_att_f).astype(jnp.bfloat16)
        d_qkv = jnp.stack([d_query, d_key, d_value], axis=1).reshape(SEQ, 3, N_MP, group_width)
        d_qkv_f = d_qkv.astype(jnp.float32)
        qkv_grad = jnp.einsum('sd,scgh->dcgh', normed.astype(jnp.float32), d_qkv_f).reshape(D, 3, HEADS * HD)
        dn_parts = jnp.einsum('scgh,dcgh->gsd', d_qkv_f, w_groups)
        dn_parts = lax.optimization_barrier(dn_parts.astype(jnp.bfloat16)).astype(jnp.float32)
        d_normed = lax.optimization_barrier(jnp.sum(dn_parts, axis=0))
        scaled = d_normed * gain_f
        d_stream = cot_s.astype(jnp.float32) + inv_std * (scaled - lax.optimization_barrier(jnp.mean(scaled, axis=-1, keepdims=True)) - unit * lax.optimization_barrier(jnp.mean(scaled * unit, axis=-1, keepdims=True)))
        return ((qkv_total + qkv_grad, out_total + out_grad), (output_s, d_stream.astype(jnp.bfloat16)))
    start_totals = (jnp.zeros((D, 3, HEADS * HD), jnp.float32), jnp.zeros((HEADS * HD, D), jnp.float32))
    slot_inputs = (stream.reshape(N_DP, SEQ, D), segment.reshape(N_DP, SEQ), cotangent.reshape(N_DP, SEQ, D))
    totals, stacked = lax.scan(slot_step, start_totals, slot_inputs)
    coef = TOTAL ** (-0.5)
    output = stacked[0].reshape(TOTAL, D)
    d_stream_all = stacked[1].reshape(TOTAL, D)
    d_patches = jnp.take(d_stream_all, target, axis=0)
    return (output, d_patches, totals[0] * coef, totals[1] * coef)
```

```python
import jax
import jax.numpy as jnp
from jax import lax
from jax.experimental import pallas as pl
from jax.experimental.pallas import tpu as pltpu
from jax.sharding import PartitionSpec as P

HD = 104
HP = 128
NH = 4
D = 1664
RD = 256
SEQ = 1024
CAP = 16
NDP = 32
SLOTS = NDP * CAP
CA = 896
MESH = pl.DeviceIdType.MESH
F32 = jnp.float32
BF = jnp.bfloat16
VM = pl.BlockSpec(memory_space=pltpu.VMEM)
BLOCKS = ((0, 0, 256, 0), (256, 256, 768, 256), (512, 256, 1024, 768), (768, 512, 1024, 1536))


def mm(a, b, ca=1, cb=0):
    return lax.dot_general(a, b, (((ca,), (cb,)), ((), ())), preferred_element_type=F32)


def rows(start, size):
    return pl.ds(pl.multiple_of(start, 16), size)


def place():
    dp, mp = lax.axis_index("dp"), lax.axis_index("mp")
    return dp, mp, lax.rem(mp + 1, 4), lax.rem(mp + 3, 4), lax.rem(mp + 2, 4)


def copier(ssem, rsem):
    def make(src, dst, n, dev):
        return pltpu.make_async_remote_copy(
            src, dst, ssem.at[n], rsem.at[n], device_id=dev, device_id_type=MESH
        )

    return make


def greet(devs):
    bar = pltpu.get_barrier_semaphore()
    for dev in devs:
        pl.semaphore_signal(bar, inc=1, device_id=dev, device_id_type=MESH)
    return bar


def greet_dp(dp, mp, right, left):
    bar = greet(((dp, right), (dp, left)))

    def one(i, carry):
        pl.semaphore_signal(
            bar, inc=1, device_id=(lax.rem(dp + i, NDP), mp), device_id_type=MESH
        )
        return carry

    lax.fori_loop(1, NDP, one, 0)
    return bar


def a2a_copies(src, dst, ssem, rsem, dp, mp):
    def make(i):
        d = lax.rem(dp + i, NDP)
        return pltpu.make_async_remote_copy(
            src.at[rows(d * CAP, CAP)],
            dst.at[rows(dp * CAP, CAP)],
            ssem.at[i],
            rsem.at[i],
            device_id=(d, mp),
            device_id_type=MESH,
        )

    def start():
        def one(i, carry):
            make(i).start()
            return carry

        lax.fori_loop(1, NDP, one, 0)
        dst[rows(dp * CAP, CAP)] = src[rows(dp * CAP, CAP)]

    def wait():
        def one(i, carry):
            make(i).wait()
            return carry

        lax.fori_loop(1, NDP, one, 0)

    return start, wait


def ring_gather(src, dst, ssem, rsem, dp, mp, right, left):
    make = copier(ssem, rsem)
    h = RD // 2

    def at(dev, half):
        return dst.at[rows(dev * RD + half * h, h)]

    a0 = make(src.at[0:h], at(mp, 0), 0, (dp, right))
    b1 = make(src.at[h:RD], at(mp, 1), 1, (dp, left))
    a1 = make(src.at[h:RD], at(mp, 1), 2, (dp, right))
    b0 = make(src.at[0:h], at(mp, 0), 3, (dp, left))
    f0 = make(at(left, 0), at(left, 0), 4, (dp, right))
    f1 = make(at(right, 1), at(right, 1), 5, (dp, left))

    def start():
        for c in (a0, b1, a1, b0):
            c.start()

    def onward():
        a0.wait_recv()
        f0.start()
        b1.wait_recv()
        f1.start()

    def near():
        a1.wait_recv()
        b0.wait_recv()

    def far():
        f0.wait_recv()
        f1.wait_recv()

    def drain():
        for c in (a0, b1, a1, b0, f0, f1):
            c.wait_send()

    return start, onward, near, far, drain


def dispatch_kernel(
    patch, pack_col, pack_row, coords, pos, gain, wq, wo, cot,
    stream, ng, cotg, qkv, datt, idx, sel,
    send, recv, as_, ar, cs, cr, ns, nr,
):
    dp, mp, right, left, opp = place()
    bar = greet_dp(dp, mp, right, left)
    g_col, g_row = pack_col[:, 0:1], pack_row[0:1, :]
    src_i = lax.broadcasted_iota(jnp.int32, (RD, RD), 0)
    dst_i = lax.broadcasted_iota(jnp.int32, (RD, RD), 1)
    before = jnp.where((g_col == g_row) & (src_i < dst_i), 1.0, 0.0)
    rank = jnp.sum(before, axis=0, keepdims=True).astype(jnp.int32)
    placed = g_row * CAP + rank
    ext = jnp.broadcast_to((pack_col[:, 1:2] + 1).astype(F32), (RD, 128)).astype(BF)

    def fill(i, carry):
        at = rows(i * 128, 128)
        slot = lax.broadcasted_iota(jnp.int32, (128, RD), 0) + i * 128
        pick = jnp.where(slot == placed, 1.0, 0.0).astype(BF)
        sel[at, :] = pick
        send[at, 0:D] = mm(pick, patch[...]).astype(BF)
        send[at, D:] = mm(pick, ext).astype(BF)
        return carry

    lax.fori_loop(0, SLOTS // 128, fill, 0)
    pl.semaphore_wait(bar, NDP + 1)
    go, done = a2a_copies(send, recv, as_, ar, dp, mp)
    c_start, c_onward, c_near, c_far, c_drain = ring_gather(
        cot, cotg, cs, cr, dp, mp, right, left
    )
    go()
    c_start()
    cotg[rows(mp * RD, RD)] = cot[...]
    c_onward()
    done()
    code = recv[:, D:].astype(F32)
    idx[...] = recv[:, D:]

    def unpack(i, carry):
        at = rows(i * 64, 64)
        want = (lax.broadcasted_iota(jnp.int32, (SLOTS, 128), 1) + 1).astype(F32)
        pick = jnp.where(code == want + (i * 128).astype(F32), 1.0, 0.0).astype(BF)
        at = rows(i * 128, 128)
        packed = mm(pick, recv[:, 0:D], 0, 0)
        gi = lax.broadcasted_iota(jnp.int32, (128, 32), 1)
        cr_ = coords[at, 0:1]
        cc_ = coords[at, 1:2] + 16
        hot = jnp.where((gi == cr_) | (gi == cc_), 1.0, 0.0).astype(BF)
        s = (packed.astype(BF).astype(F32) + mm(hot, pos[...])).astype(BF)
        stream[at, :] = s
        sf = s.astype(F32)
        cen = sf - jnp.mean(sf, axis=-1, keepdims=True)
        inv = lax.rsqrt(jnp.mean(cen * cen, axis=-1, keepdims=True) + 1e-06)
        ng[rows(mp * RD + i * 128, 128), :] = (cen * inv * gain[...].astype(F32)).astype(BF)
        return carry

    lax.fori_loop(0, RD // 128, unpack, 0)
    n_start, n_onward, n_near, n_far, n_drain = ring_gather(
        ng.at[rows(mp * RD, RD)], ng, ns, nr, dp, mp, right, left
    )
    n_start()

    def project(s):
        def one(n, carry):
            col = pl.ds(pl.multiple_of(n * 512, 128), 512)
            qkv[rows(s * RD, RD), col] = mm(ng[rows(s * RD, RD)], wq[:, col]).astype(BF)
            return carry

        lax.fori_loop(0, 3, one, 0)

    def back(s):
        datt[rows(s * RD, RD), :] = mm(cotg[rows(s * RD, RD)], wo[...], 1, 1).astype(BF)

    project(mp)
    back(mp)
    c_near()
    c_far()
    n_onward()
    back(right)
    back(left)
    back(opp)
    n_near()
    project(right)
    project(left)
    n_far()
    project(opp)
    c_drain()
    n_drain()


def ring_reduce(part, ha, hb, fl, fr, ssem, rsem, dp, mp, right, left, opp):
    make = copier(ssem, rsem)
    h = RD // 2

    def at(dev, half):
        return part.at[rows(dev * RD + half * h, h)]

    s0 = make(at(opp, 0), ha, 0, (dp, right))
    s1 = make(at(opp, 1), hb, 1, (dp, left))
    s2 = make(at(right, 1), fl.at[h:RD], 2, (dp, right))
    s3 = make(at(left, 0), fr.at[0:h], 3, (dp, left))
    s4 = make(at(right, 0), fl.at[0:h], 4, (dp, right))
    s5 = make(at(left, 1), fr.at[h:RD], 5, (dp, left))

    def first():
        s0.start()
        s1.start()

    def second():
        s2.start()
        s3.start()

    def onward():
        s0.wait_recv()
        r0 = rows(right * RD, h)
        part[r0] = (part[r0].astype(F32) + ha[...].astype(F32)).astype(BF)
        s4.start()
        s1.wait_recv()
        r1 = rows(left * RD + h, h)
        part[r1] = (part[r1].astype(F32) + hb[...].astype(F32)).astype(BF)
        s5.start()

    def finish():
        for c in (s2, s3, s4, s5):
            c.wait_recv()

    def drain():
        for c in (s0, s1, s2, s3, s4, s5):
            c.wait_send()

    return first, second, onward, finish, drain


def attention_kernel(
    scal, qkv, datt, ng, cotg, seg_col, seg_row, wq, wo, stream,
    grad, dnp, out,
    prob, att, dqkv, dk, dv, part, ha, hb, fl, fr, ss, sr,
):
    dp, mp, right, left, opp = place()
    bar = greet(((dp, right), (dp, left)))
    scale = HD ** (-0.5)
    coef = scal[0]

    def fwd(h, carry):
        base = h * 3 * HP
        qc = pl.ds(pl.multiple_of(base, 128), HP)
        kc = pl.ds(pl.multiple_of(base + HP, 128), HP)
        vc = pl.ds(pl.multiple_of(base + 2 * HP, 128), HP)
        for r0, k0, k1, p0 in BLOCKS:
            s = mm(qkv[r0 : r0 + 256, qc], qkv[k0:k1, kc], 1, 1) * scale
            same = seg_col[r0 : r0 + 256, :] == seg_row[:, k0:k1]
            s = jnp.where(same, s, -1e30)
            e = jnp.where(same, jnp.exp(s - jnp.max(s, axis=-1, keepdims=True)), 0.0)
            p = (e / jnp.sum(e, axis=-1, keepdims=True)).astype(BF)
            prob[h, :, p0 : p0 + k1 - k0] = p
            hc = pl.ds(pl.multiple_of(h * HP, 128), HP)
            att[r0 : r0 + 256, hc] = mm(p, qkv[k0:k1, vc]).astype(BF)
        return carry

    lax.fori_loop(0, NH, fwd, 0)
    first, second, onward, finish, drain = ring_reduce(
        part, ha, hb, fl, fr, ss, sr, dp, mp, right, left, opp
    )

    def project(s):
        part[rows(s * RD, RD), :] = mm(att[rows(s * RD, RD), :], wo[...]).astype(BF)

    project(opp)
    pl.semaphore_wait(bar, 2)
    first()
    project(right)
    project(left)
    second()
    project(mp)

    def bwd(h, carry):
        base = h * 3 * HP
        qc = pl.ds(pl.multiple_of(base, 128), HP)
        kc = pl.ds(pl.multiple_of(base + HP, 128), HP)
        vc = pl.ds(pl.multiple_of(base + 2 * HP, 128), HP)
        hc = pl.ds(pl.multiple_of(h * HP, 128), HP)
        dk[...] = jnp.zeros_like(dk)
        dv[...] = jnp.zeros_like(dv)
        for r0, k0, k1, p0 in BLOCKS:
            p = prob[h, :, p0 : p0 + k1 - k0]
            da = datt[r0 : r0 + 256, hc]
            delta = jnp.sum(
                da.astype(F32) * att[r0 : r0 + 256, hc].astype(F32), axis=-1, keepdims=True
            )
            dprob = mm(da, qkv[k0:k1, vc], 1, 1)
            ds = (p.astype(F32) * (dprob - delta) * scale).astype(BF)
            dqkv[r0 : r0 + 256, qc] = mm(ds, qkv[k0:k1, kc]).astype(BF)
            dk[k0:k1, :] += mm(ds, qkv[r0 : r0 + 256, qc], 0, 0)
            dv[k0:k1, :] += mm(p, da, 0, 0)
        dqkv[:, kc] = dk[...].astype(BF)
        dqkv[:, vc] = dv[...].astype(BF)
        all3 = pl.ds(pl.multiple_of(base, 128), 3 * HP)
        grad[rows(h * 512, 384), :] = (mm(dqkv[:, all3], ng[...], 0, 0) * coef).astype(BF)
        grad[rows(h * 512 + 384, 128), :] = (mm(att[:, hc], cotg[...], 0, 0) * coef).astype(BF)

        @pl.when(h == 1)
        def _():
            onward()

        return carry

    lax.fori_loop(0, NH, bwd, 0)

    def d_rows(s, carry):
        dnp[rows(s * RD, RD), :] = mm(dqkv[rows(s * RD, RD), :], wq[...], 1, 1).astype(BF)
        return carry

    lax.fori_loop(0, 4, d_rows, 0)
    finish()
    total = part[rows(mp * RD, RD)].astype(F32) + fl[...].astype(F32) + fr[...].astype(F32)
    out[...] = (stream[...].astype(F32) + total).astype(BF)
    drain()


def reduce_kernel(
    grad, dnp_in, stream, cot, idx, sel, gain,
    total, dpatch,
    dnp, ha, hb, fl, fr, core_in, mine, ax, az, bx, bz, asum, bsum, back, ret, dstream,
    ys, yr, gs, gr, as_, ar,
):
    dp, mp, right, left, opp = place()
    bar = greet_dp(dp, mp, right, left)
    c = lax.rem(dp, 2)
    x = lax.rem(dp // 2, 4)
    z = dp // 8
    make = copier(gs, gr)
    other = 1 - c

    def dev(zz, xx, cc):
        return ((zz * 4 + xx) * 2 + cc, mp)

    def shift(v, s):
        return lax.rem(v + s, 4)

    dnp[...] = dnp_in[...]
    pl.semaphore_wait(bar, NDP + 1)
    first, second, onward, finish, drain = ring_reduce(
        dnp, ha, hb, fl, fr, ys, yr, dp, mp, right, left, opp
    )
    first()
    second()
    swap = make(grad.at[rows(other * 1024, 1024)], core_in, 0, dev(z, x, other))
    swap.start()
    swap.wait_recv()

    def add_core(i, carry):
        r = rows(i * 128, 128)
        g = grad[rows(c * 1024 + i * 128, 128)].astype(F32)
        mine[r, :] = (g + core_in[r, :].astype(F32)).astype(BF)
        return carry

    lax.fori_loop(0, 8, add_core, 0)
    a_cols, b_cols = pl.ds(0, CA), pl.ds(CA, D - CA)
    a1 = [make(mine.at[rows(shift(x, s) * 256, 256), a_cols], ax.at[s - 1], s, dev(z, shift(x, s), c)) for s in (1, 2, 3)]
    b1 = [make(mine.at[rows(shift(z, s) * 256, 256), b_cols], bx.at[s - 1], 3 + s, dev(shift(z, s), x, c)) for s in (1, 2, 3)]
    for s in (1, 0, 2):
        a1[s].start()
        b1[s].start()
    onward()
    for q in a1:
        q.wait_recv()
    asum[...] = (
        mine[rows(x * 256, 256), a_cols].astype(F32)
        + ax[0].astype(F32)
        + ax[1].astype(F32)
        + ax[2].astype(F32)
    ).astype(BF)
    a2 = [make(asum.at[rows(shift(z, s) * 64, 64)], az.at[s - 1], 6 + s, dev(shift(z, s), x, c)) for s in (1, 2, 3)]
    for q in a2:
        q.start()
    for q in b1:
        q.wait_recv()
    bsum[...] = (
        mine[rows(z * 256, 256), b_cols].astype(F32)
        + bx[0].astype(F32)
        + bx[1].astype(F32)
        + bx[2].astype(F32)
    ).astype(BF)
    b2 = [make(bsum.at[rows(shift(x, s) * 64, 64)], bz.at[s - 1], 9 + s, dev(z, shift(x, s), c)) for s in (1, 2, 3)]
    for q in b2:
        q.start()
    for q in a2:
        q.wait_recv()
    ra = rows(c * 1024 + x * 256 + z * 64, 64)
    total[ra, a_cols] = (
        asum[rows(z * 64, 64), :].astype(F32)
        + az[0].astype(F32)
        + az[1].astype(F32)
        + az[2].astype(F32)
    ).astype(BF)
    pa = total.at[ra, a_cols]
    a3 = [make(pa, pa, 12 + s, dev(shift(z, s), x, c)) for s in (1, 2, 3)]
    for q in a3:
        q.start()
    for q in b2:
        q.wait_recv()
    rb = rows(c * 1024 + z * 256 + x * 64, 64)
    total[rb, b_cols] = (
        bsum[rows(x * 64, 64), :].astype(F32)
        + bz[0].astype(F32)
        + bz[1].astype(F32)
        + bz[2].astype(F32)
    ).astype(BF)
    pb = total.at[rb, b_cols]
    b3 = [make(pb, pb, 15 + s, dev(z, shift(x, s), c)) for s in (1, 2, 3)]
    for q in b3:
        q.start()

    finish()
    go, done = a2a_copies(back, ret, as_, ar, dp, mp)

    def ln_back(i, carry):
        r = rows(i * 64, 64)
        sf = stream[r, :].astype(F32)
        cen = sf - jnp.mean(sf, axis=-1, keepdims=True)
        inv = lax.rsqrt(jnp.mean(cen * cen, axis=-1, keepdims=True) + 1e-06)
        unit = cen * inv
        dn = dnp[rows(mp * RD + i * 64, 64), :].astype(F32)
        e = (dn + fl[r, :].astype(F32) + fr[r, :].astype(F32)) * gain[...].astype(F32)
        dst = cot[r, :].astype(F32) + inv * (
            e
            - jnp.mean(e, axis=-1, keepdims=True)
            - unit * jnp.mean(e * unit, axis=-1, keepdims=True)
        )
        dstream[r, :] = dst.astype(BF)
        return carry

    lax.fori_loop(0, RD // 64, ln_back, 0)

    def spread(i, carry):
        r = rows(i * 128, 128)
        code = idx[r, :].astype(F32)
        want = (lax.broadcasted_iota(jnp.int32, (128, 128), 1) + 1).astype(F32)
        lo = jnp.where(code == want, 1.0, 0.0).astype(BF)
        hi = jnp.where(code == want + 128.0, 1.0, 0.0).astype(BF)
        back[r, :] = (mm(lo, dstream[0:128, :]) + mm(hi, dstream[128:256, :])).astype(BF)
        return carry

    lax.fori_loop(0, SLOTS // 128, spread, 0)
    for q in a3:
        q.wait_recv()
    qa = total.at[rows(c * 1024 + x * 256, 256), a_cols]
    a4 = [make(qa, qa, 18 + s, dev(z, shift(x, s), c)) for s in (1, 2, 3)]
    for q in a4:
        q.start()
    for q in b3:
        q.wait_recv()
    qb = total.at[rows(c * 1024 + z * 256, 256), b_cols]
    b4 = [make(qb, qb, 21 + s, dev(shift(z, s), x, c)) for s in (1, 2, 3)]
    for q in b4:
        q.start()
    go()
    for q in a4 + b4:
        q.wait_recv()
    half = total.at[rows(c * 1024, 1024)]
    last = make(half, half, 25, dev(z, x, other))
    last.start()
    done()

    def collect(i, carry):
        r = rows(i * 128, 128)
        col = pl.ds(pl.multiple_of(i * 128, 128), 128)
        dpatch[r, :] = mm(sel[:, col], ret[...], 0, 0).astype(BF)
        return carry

    lax.fori_loop(0, RD // 128, collect, 0)
    last.wait_recv()
    drain()
    for q in [swap, last] + a1 + b1 + a2 + b2 + a3 + b3 + a4 + b4:
        q.wait_send()


def sds(*shape):
    return jax.ShapeDtypeStruct(shape, BF)


def vm(*shape):
    return pltpu.VMEM(shape, BF)


def params(n):
    return pltpu.CompilerParams(
        collective_id=n, has_side_effects=True, vmem_limit_bytes=60 * 2**20
    )


def dma(n):
    return pltpu.SemaphoreType.DMA((n,))


def local(
    patch_rows, packing, segment, coords, pos_rows, pos_cols, norm_gain, w_qkv, w_out, cotangent
):
    total_rows = RD * lax.axis_size("dp") * lax.axis_size("mp")
    coef = jnp.full((1,), total_rows ** (-0.5), F32)
    wq = jnp.pad(
        w_qkv.reshape(D, 3, NH, HD).transpose(0, 2, 1, 3), ((0, 0), (0, 0), (0, 0), (0, HP - HD))
    ).reshape(D, NH * 3 * HP)
    wo = jnp.pad(w_out.reshape(NH, HD, D), ((0, 0), (0, HP - HD), (0, 0))).reshape(NH * HP, D)
    pos = jnp.concatenate([pos_rows, pos_cols], axis=0)
    gain = norm_gain.reshape(1, D)
    stream, ng, cotg, qkv, datt, idx, sel = pl.pallas_call(
        dispatch_kernel,
        out_shape=(
            sds(RD, D), sds(SEQ, D), sds(SEQ, D), sds(SEQ, NH * 3 * HP), sds(SEQ, NH * HP),
            sds(SLOTS, 128), sds(SLOTS, RD),
        ),
        in_specs=[VM] * 9,
        out_specs=[VM] * 7,
        scratch_shapes=[
            vm(SLOTS, D + 128), vm(SLOTS, D + 128),
            dma(NDP), dma(NDP), dma(6), dma(6), dma(6), dma(6),
        ],
        compiler_params=params(0),
        name="dispatch",
    )(patch_rows, packing.T, packing, coords.T, pos, gain, wq, wo, cotangent)
    h = RD // 2
    grad, dnp, output = pl.pallas_call(
        attention_kernel,
        out_shape=(sds(NH * 512, D), sds(SEQ, D), sds(RD, D)),
        in_specs=[pl.BlockSpec(memory_space=pltpu.SMEM)] + [VM] * 9,
        out_specs=[VM] * 3,
        scratch_shapes=[
            vm(NH, 256, 2048), vm(SEQ, NH * HP), vm(SEQ, NH * 3 * HP),
            pltpu.VMEM((SEQ, HP), F32), pltpu.VMEM((SEQ, HP), F32),
            vm(SEQ, D), vm(h, D), vm(h, D), vm(RD, D), vm(RD, D), dma(6), dma(6),
        ],
        compiler_params=params(1),
        name="attention",
    )(coef, qkv, datt, ng, cotg, segment.reshape(SEQ, 1), segment.reshape(1, SEQ), wq, wo, stream)
    total, d_patches = pl.pallas_call(
        reduce_kernel,
        out_shape=(sds(NH * 512, D), sds(RD, D)),
        in_specs=[VM] * 7,
        out_specs=[VM] * 2,
        scratch_shapes=[
            vm(SEQ, D), vm(h, D), vm(h, D), vm(RD, D), vm(RD, D),
            vm(1024, D), vm(1024, D),
            vm(3, 256, CA), vm(3, 64, CA), vm(3, 256, D - CA), vm(3, 64, D - CA),
            vm(256, CA), vm(256, D - CA), vm(SLOTS, D), vm(SLOTS, D), vm(RD, D),
            dma(6), dma(6), dma(26), dma(26), dma(NDP), dma(NDP),
        ],
        compiler_params=params(2),
        name="reduce",
    )(grad, dnp, stream, cotangent, idx, sel, gain)
    parts = total.reshape(NH, 4, HP, D)[:, :, :HD]
    grad_qkv = parts[:, :3].transpose(3, 1, 0, 2).reshape(D, 3, NH * HD).astype(F32)
    grad_out = parts[:, 3].reshape(NH * HD, D).astype(F32)
    return (output, d_patches, grad_qkv, grad_out)


def solution(mesh):
    placed = (
        P(("dp", "mp"), None),
        P(None, ("dp", "mp")),
        P("dp"),
        P(None, ("dp", "mp")),
        P(),
        P(),
        P(),
        P(None, None, "mp"),
        P("mp", None),
        P(("dp", "mp"), None),
    )
    return jax.shard_map(
        local,
        mesh=mesh,
        in_specs=placed,
        out_specs=(
            P(("dp", "mp"), None),
            P(("dp", "mp"), None),
            P(None, None, "mp"),
            P("mp", None),
        ),
        check_vma=False,
    )
```

```python
import jax
import jax.numpy as jnp
from jax import lax
from jax.experimental import pallas as pl
from jax.experimental.pallas import tpu as pltpu
from jax.sharding import PartitionSpec as P

HD = 104
HP = 128
NH = 4
D = 1664
RD = 256
SEQ = 1024
CAP = 16
NDP = 32
SLOTS = NDP * CAP
CA = 896
GW = NH * HD
MESH = pl.DeviceIdType.MESH
F32 = jnp.float32
BF = jnp.bfloat16
VM = pl.BlockSpec(memory_space=pltpu.VMEM)
BLOCKS = ((0, 0, 256, 0), (256, 256, 768, 256), (512, 256, 1024, 768), (768, 512, 1024, 1536))


def mm(a, b, ca=1, cb=0):
    return lax.dot_general(a, b, (((ca,), (cb,)), ((), ())), preferred_element_type=F32)


def rows(start, size):
    return pl.ds(pl.multiple_of(start, 16), size)


def place():
    dp, mp = lax.axis_index("dp"), lax.axis_index("mp")
    return dp, mp, lax.rem(mp + 1, 4), lax.rem(mp + 3, 4), lax.rem(mp + 2, 4)


def copier(ssem, rsem):
    def make(src, dst, n, dev):
        return pltpu.make_async_remote_copy(
            src, dst, ssem.at[n], rsem.at[n], device_id=dev, device_id_type=MESH
        )

    return make


def greet(devs):
    bar = pltpu.get_barrier_semaphore()
    for dev in devs:
        pl.semaphore_signal(bar, inc=1, device_id=dev, device_id_type=MESH)
    return bar


def greet_dp(dp, mp, right, left):
    bar = greet(((dp, right), (dp, left)))

    def one(i, carry):
        pl.semaphore_signal(
            bar, inc=1, device_id=(lax.rem(dp + i, NDP), mp), device_id_type=MESH
        )
        return carry

    lax.fori_loop(1, NDP, one, 0)
    return bar


def a2a_copies(src, dst, ssem, rsem, dp, mp, width=D + 128):
    def make(i):
        d = lax.rem(dp + i, NDP)
        return pltpu.make_async_remote_copy(
            src.at[rows(d * CAP, CAP), 0:width],
            dst.at[rows(dp * CAP, CAP), 0:width],
            ssem.at[i],
            rsem.at[i],
            device_id=(d, mp),
            device_id_type=MESH,
        )

    def start():
        def one(i, carry):
            make(i).start()
            return carry

        lax.fori_loop(1, NDP, one, 0)
        dst[rows(dp * CAP, CAP), 0:width] = src[rows(dp * CAP, CAP), 0:width]

    def wait():
        def one(i, carry):
            make(i).wait()
            return carry

        lax.fori_loop(1, NDP, one, 0)

    return start, wait


def ring_gather(src, dst, ssem, rsem, dp, mp, right, left):
    make = copier(ssem, rsem)
    h = RD // 2

    def at(dev, half):
        return dst.at[rows(dev * RD + half * h, h)]

    a0 = make(src.at[0:h], at(mp, 0), 0, (dp, right))
    b1 = make(src.at[h:RD], at(mp, 1), 1, (dp, left))
    a1 = make(src.at[h:RD], at(mp, 1), 2, (dp, right))
    b0 = make(src.at[0:h], at(mp, 0), 3, (dp, left))
    f0 = make(at(left, 0), at(left, 0), 4, (dp, right))
    f1 = make(at(right, 1), at(right, 1), 5, (dp, left))

    def start():
        for c in (a0, b1, a1, b0):
            c.start()

    def onward():
        a0.wait_recv()
        f0.start()
        b1.wait_recv()
        f1.start()

    def near():
        a1.wait_recv()
        b0.wait_recv()

    def far():
        f0.wait_recv()
        f1.wait_recv()

    def drain():
        for c in (a0, b1, a1, b0, f0, f1):
            c.wait_send()

    return start, onward, near, far, drain


def ring_reduce(part, ha, hb, fl, fr, ssem, rsem, dp, mp, right, left, opp):
    make = copier(ssem, rsem)
    h = RD // 2

    def at(dev, half):
        return part.at[rows(dev * RD + half * h, h)]

    s0 = make(at(opp, 0), ha, 0, (dp, right))
    s1 = make(at(opp, 1), hb, 1, (dp, left))
    s2 = make(at(right, 1), fl.at[h:RD], 2, (dp, right))
    s3 = make(at(left, 0), fr.at[0:h], 3, (dp, left))
    s4 = make(at(right, 0), fl.at[0:h], 4, (dp, right))
    s5 = make(at(left, 1), fr.at[h:RD], 5, (dp, left))

    def first():
        s0.start()
        s1.start()

    def second():
        s2.start()
        s3.start()

    def onward():
        s0.wait_recv()
        r0 = rows(right * RD, h)
        part[r0] = (part[r0].astype(F32) + ha[...].astype(F32)).astype(BF)
        s4.start()
        s1.wait_recv()
        r1 = rows(left * RD + h, h)
        part[r1] = (part[r1].astype(F32) + hb[...].astype(F32)).astype(BF)
        s5.start()

    def finish():
        for c in (s2, s3, s4, s5):
            c.wait_recv()

    def drain():
        for c in (s0, s1, s2, s3, s4, s5):
            c.wait_send()

    return first, second, onward, finish, drain


def column(row):
    n = row.shape[1]
    eye = lax.broadcasted_iota(jnp.int32, (n, n), 0) == lax.broadcasted_iota(jnp.int32, (n, n), 1)
    return jnp.sum(jnp.where(eye, row.astype(F32), 0.0), axis=1, keepdims=True).astype(jnp.int32)


def layer_norm(stream_rows):
    sf = stream_rows.astype(F32)
    cen = sf - jnp.mean(sf, axis=-1, keepdims=True)
    inv = lax.rsqrt(jnp.mean(cen * cen, axis=-1, keepdims=True) + 1e-06)
    return cen * inv, inv


def head_cols(h):
    base = h * 3 * HP
    return [pl.ds(pl.multiple_of(base + k * HP, 128), HP) for k in range(3)]


def sublayer_kernel(
    packing, coords, seg, prow, pcol, gain, patch_in, w_in, wo_in, cot_in,
    out, dpatch, total,
    stream, ng, cotg, qkv, datt, idx, sel, wq, wo, crd, segc,
    send, recv, ret, prob, att, dk, dv, part, dnp, grad,
    ha, hb, fl, fr, ha2, hb2, fl2, fr2, core_in, ax, az, bx, bz,
    as_, ar, bs, br, cs, cr, ns, nr, os_, or_, ys, yr, gs, gr, ls, lk,
):
    dp, mp, right, left, opp = place()
    c = lax.rem(dp, 2)
    x = lax.rem(dp // 2, 4)
    z = dp // 8
    other = 1 - c
    scale = HD ** (-0.5)
    coef = (RD * NDP * 4) ** (-0.5)
    bar = greet_dp(dp, mp, right, left)
    l_w = pltpu.make_async_copy(w_in, grad.at[0:3, 0:GW], ls.at[0])
    l_o = pltpu.make_async_copy(wo_in, grad.at[3, 0:GW], ls.at[1])
    l_c = pltpu.make_async_copy(cot_in, cotg.at[rows(mp * RD, RD)], ls.at[2])
    patch = part.at[0:RD]
    l_p = pltpu.make_async_copy(patch_in, patch, ls.at[7])
    l_p.start()
    l_c.start()
    l_w.start()
    l_o.start()

    g_row = packing[0:1, :]
    src_i = lax.broadcasted_iota(jnp.int32, (RD, RD), 0)
    dst_i = lax.broadcasted_iota(jnp.int32, (RD, RD), 1)
    before = jnp.where((column(g_row) == g_row) & (src_i < dst_i), 1.0, 0.0)
    rank = jnp.sum(before, axis=0, keepdims=True).astype(jnp.int32)
    placed = g_row * CAP + rank
    ext = jnp.broadcast_to((column(packing[1:2, :]) + 1).astype(F32), (RD, 128)).astype(BF)

    l_p.wait()

    def fill(i, carry):
        at = rows(i * 128, 128)
        slot = lax.broadcasted_iota(jnp.int32, (128, RD), 0) + i * 128
        pick = jnp.where(slot == placed, 1.0, 0.0).astype(BF)
        sel[at, :] = pick
        send[at, 0:D] = mm(pick, patch[...]).astype(BF)
        send[at, D:] = mm(pick, ext).astype(BF)
        return carry

    lax.fori_loop(0, SLOTS // 128, fill, 0)
    pl.semaphore_wait(bar, NDP + 1)
    go, done = a2a_copies(send, recv, as_, ar, dp, mp)
    go()
    l_c.wait()
    c_start, c_onward, c_near, c_far, c_drain = ring_gather(
        cotg.at[rows(mp * RD, RD)], cotg, cs, cr, dp, mp, right, left
    )
    c_start()

    crd[:, 0:1] = column(coords[0:1, :])
    crd[:, 1:2] = column(coords[1:2, :])
    for i in range(4):
        segc[i * 256 : (i + 1) * 256, :] = column(seg[:, i * 256 : (i + 1) * 256])
    l_w.wait()
    l_o.wait()

    def pad_head(h, carry):
        i0 = lax.broadcasted_iota(jnp.int32, (HP, GW), 0)
        i1 = lax.broadcasted_iota(jnp.int32, (HP, GW), 1)
        pick = jnp.where((i1 == i0 + h * HD) & (i0 < HD), 1.0, 0.0).astype(BF)

        def one(k, inner):
            wq[rows(h * 3 * HP + k * HP, HP), :] = mm(pick, grad[k, 0:GW, :]).astype(BF)
            return inner

        lax.fori_loop(0, 3, one, 0)
        wo[rows(h * HP, HP), :] = mm(pick, grad[3, 0:GW, :]).astype(BF)
        return carry

    lax.fori_loop(0, NH, pad_head, 0)
    c_onward()
    done()
    idx[...] = recv[:, D:]

    def unpack(i, carry):
        at = rows(i * 128, 128)
        code = recv[:, D:].astype(F32)
        want = (lax.broadcasted_iota(jnp.int32, (SLOTS, 128), 1) + (i * 128 + 1)).astype(F32)
        pick = jnp.where(code == want, 1.0, 0.0).astype(BF)
        packed = mm(pick, recv[:, 0:D], 0, 0)
        gi = lax.broadcasted_iota(jnp.int32, (128, 16), 1)
        row_hot = jnp.where(gi == crd[at, 0:1], 1.0, 0.0).astype(BF)
        col_hot = jnp.where(gi == crd[at, 1:2], 1.0, 0.0).astype(BF)
        s = (packed + mm(row_hot, prow[...]) + mm(col_hot, pcol[...])).astype(BF)
        stream[at, :] = s
        unit, _ = layer_norm(s)
        ng[rows(mp * RD + i * 128, 128), :] = (unit * gain[...].astype(F32)).astype(BF)
        return carry

    lax.fori_loop(0, RD // 128, unpack, 0)
    n_start, n_onward, n_near, n_far, n_drain = ring_gather(
        ng.at[rows(mp * RD, RD)], ng, ns, nr, dp, mp, right, left
    )
    n_start()

    def project(s):
        def one(n, carry):
            col = pl.ds(pl.multiple_of(n * 512, 128), 512)
            qkv[rows(s * RD, RD), col] = mm(
                ng[rows(s * RD, RD)], wq[rows(n * 512, 512), :], 1, 1
            ).astype(BF)
            return carry

        lax.fori_loop(0, 3, one, 0)

    def back_project(s):
        datt[rows(s * RD, RD), :] = mm(cotg[rows(s * RD, RD)], wo[...], 1, 1).astype(BF)

    project(mp)
    back_project(mp)
    c_near()
    c_far()
    back_project(right)
    back_project(left)
    back_project(opp)
    n_onward()
    n_near()
    project(right)
    project(left)
    n_far()
    project(opp)

    def fwd(h, carry):
        qc, kc, vc = head_cols(h)
        hc = pl.ds(pl.multiple_of(h * HP, 128), HP)
        for r0, k0, k1, p0 in BLOCKS:
            s = mm(qkv[r0 : r0 + 256, qc], qkv[k0:k1, kc], 1, 1) * scale
            same = segc[r0 : r0 + 256, :] == seg[:, k0:k1]
            s = jnp.where(same, s, -1e30)
            e = jnp.where(same, jnp.exp(s - jnp.max(s, axis=-1, keepdims=True)), 0.0)
            p = (e / jnp.sum(e, axis=-1, keepdims=True)).astype(BF)
            prob[h, :, p0 : p0 + k1 - k0] = p
            att[r0 : r0 + 256, hc] = mm(p, qkv[k0:k1, vc]).astype(BF)
        return carry

    lax.fori_loop(0, NH, fwd, 0)
    first, second, onward, finish, drain = ring_reduce(
        part, ha, hb, fl, fr, os_, or_, dp, mp, right, left, opp
    )

    def out_rows(s):
        part[rows(s * RD, RD), :] = mm(att[rows(s * RD, RD), :], wo[...]).astype(BF)

    out_rows(opp)
    first()
    out_rows(right)
    out_rows(left)
    second()
    out_rows(mp)

    def dev(zz, xx, cc):
        return ((zz * 4 + xx) * 2 + cc, mp)

    def shift(v, s):
        return lax.rem(v + s, 4)

    halves = (pl.ds(0, CA), pl.ds(CA, D - CA))

    def piece(h, r, size, cols):
        return grad.at[2 * c + r // HP, rows(h * HP + lax.rem(r, HP), size), cols]

    def placed_piece(h, r, size, cols):
        return total.at[2 * c + r // HP, rows(h * HP + lax.rem(r, HP), size), cols]

    class Stage:
        def __init__(self, h):
            def make(src, dst, n, to):
                return pltpu.make_async_remote_copy(
                    src, dst, gs.at[h, n], gr.at[h, n], device_id=to, device_id_type=MESH
                )

            def far(axis, s):
                return dev(z, shift(x, s), c) if axis == 0 else dev(shift(z, s), x, c)

            self.h = h
            self.make, self.far = make, far

        def swap(self):
            hr = rows(self.h * HP, HP)
            return self.make(
                grad.at[pl.ds(2 * other, 2), hr], core_in.at[self.h], 0, dev(z, x, other)
            )

        def last(self):
            ours = total.at[pl.ds(2 * c, 2), rows(self.h * HP, HP)]
            return self.make(ours, ours, 25, dev(z, x, other))

        def group(self, kind, a):
            one, two = (x, z) if a == 0 else (z, x)
            copies = []
            for s in (1, 2, 3):
                if kind == 0:
                    src = piece(self.h, shift(one, s) * 64, 64, halves[a])
                    dst = (ax, bx)[a].at[self.h, s - 1]
                elif kind == 1:
                    src = piece(self.h, one * 64 + shift(two, s) * 16, 16, halves[a])
                    dst = (az, bz)[a].at[self.h, s - 1]
                elif kind == 2:
                    src = piece(self.h, one * 64 + two * 16, 16, halves[a])
                    dst = placed_piece(self.h, one * 64 + two * 16, 16, halves[a])
                else:
                    src = dst = placed_piece(self.h, one * 64, 64, halves[a])
                axis = a if kind in (0, 3) else 1 - a
                copies.append(self.make(src, dst, 12 * a + 3 * kind + s, self.far(axis, s)))
            return copies

        def keep(self, a):
            one, two = (x, z) if a == 0 else (z, x)
            r = one * 64 + two * 16
            return pltpu.make_async_copy(
                piece(self.h, r, 16, halves[a]),
                placed_piece(self.h, r, 16, halves[a]),
                lk.at[self.h, a],
            )

        def s0(self):
            self.swap().start()

        def s1(self):
            h = self.h
            self.swap().wait_recv()
            hr = rows(h * HP, HP)
            for k in range(2):
                mine = grad[2 * c + k, hr, :].astype(F32)
                grad[2 * c + k, hr, :] = (mine + core_in[h, k].astype(F32)).astype(BF)
            big = self.group(0, 0), self.group(0, 1)
            for s in (1, 0, 2):
                for a in range(2):
                    big[a][s].start()

        def gather(self, copies, ref, incoming, nxt):
            for q in copies:
                q.wait_recv()
            val = ref[...].astype(F32)
            for s in range(3):
                val += incoming[self.h, s].astype(F32)
            ref[...] = val.astype(BF)
            for q in nxt:
                q.start()

        def s2(self):
            for a, b_in in enumerate((ax, bx)):
                one = x if a == 0 else z
                ref = piece(self.h, one * 64, 64, halves[a])
                self.gather(self.group(0, a), ref, b_in, self.group(1, a))

        def s3(self):
            for a, s_in in enumerate((az, bz)):
                one, two = (x, z) if a == 0 else (z, x)
                ref = piece(self.h, one * 64 + two * 16, 16, halves[a])
                self.gather(self.group(1, a), ref, s_in, self.group(2, a) + [self.keep(a)])

        def s4(self):
            for a in range(2):
                self.keep(a).wait()
                for q in self.group(2, a):
                    q.wait_recv()
                for q in self.group(3, a):
                    q.start()

        def s5(self):
            for a in range(2):
                for q in self.group(3, a):
                    q.wait_recv()
            self.last().start()

        def s6(self):
            self.last().wait_recv()

        def s7(self):
            sent = [self.swap(), self.last()]
            for kind in range(4):
                sent += self.group(kind, 0) + self.group(kind, 1)
            for q in sent:
                q.wait_send()

    def weight_grad(h):
        hr = rows(h * HP, HP)
        all3 = pl.ds(pl.multiple_of(h * 3 * HP, 128), 3 * HP)
        g = (mm(qkv[:, all3], ng[...], 0, 0) * coef).astype(BF)
        for k in range(3):
            grad[k, hr, :] = g[k * HP : (k + 1) * HP]
        hc = pl.ds(pl.multiple_of(h * HP, 128), HP)
        grad[3, hr, :] = (mm(att[:, hc], cotg[...], 0, 0) * coef).astype(BF)
        Stage(h).s0()

    def bwd(h, carry):
        qc, kc, vc = head_cols(h)
        hc = pl.ds(pl.multiple_of(h * HP, 128), HP)
        dk[...] = jnp.zeros_like(dk)
        dv[...] = jnp.zeros_like(dv)
        for r0, k0, k1, p0 in BLOCKS:
            p = prob[h, :, p0 : p0 + k1 - k0]
            da = datt[r0 : r0 + 256, hc]
            delta = jnp.sum(
                da.astype(F32) * att[r0 : r0 + 256, hc].astype(F32), axis=-1, keepdims=True
            )
            dprob = mm(da, qkv[k0:k1, vc], 1, 1)
            ds = (p.astype(F32) * (dprob - delta) * scale).astype(BF)
            dk[k0:k1, :] += mm(ds, qkv[r0 : r0 + 256, qc], 0, 0)
            dv[k0:k1, :] += mm(p, da, 0, 0)
            qkv[r0 : r0 + 256, qc] = mm(ds, qkv[k0:k1, kc]).astype(BF)
        qkv[:, kc] = dk[...].astype(BF)
        qkv[:, vc] = dv[...].astype(BF)

        @pl.when(h >= 1)
        def _():
            weight_grad(h - 1)

        @pl.when(h >= 2)
        def _():
            Stage(h - 2).s1()

        @pl.when(h == 1)
        def _():
            onward()

        @pl.when(h == 3)
        def _():
            Stage(h - 3).s2()

        return carry

    lax.fori_loop(0, NH, bwd, 0)
    first2, second2, onward2, finish2, drain2 = ring_reduce(
        dnp, ha2, hb2, fl2, fr2, ys, yr, dp, mp, right, left, opp
    )

    def d_rows(s):
        dnp[rows(s * RD, RD), :] = mm(qkv[rows(s * RD, RD), :], wq[...]).astype(BF)

    d_rows(opp)
    first2()
    d_rows(right)
    d_rows(left)
    second2()
    weight_grad(3)
    d_rows(mp)
    st = [Stage(h) for h in range(NH)]
    st[2].s1()
    onward2()
    st[1].s2()
    st[0].s3()
    st[3].s1()
    finish()
    acc = part[rows(mp * RD, RD)].astype(F32) + fl[...].astype(F32) + fr[...].astype(F32)
    part[rows(mp * RD, RD)] = (stream[...].astype(F32) + acc).astype(BF)
    l_out = pltpu.make_async_copy(part.at[rows(mp * RD, RD)], out, ls.at[8])
    l_out.start()
    st[2].s2()
    st[1].s3()
    st[0].s4()
    st[3].s2()
    st[2].s3()
    st[1].s4()
    st[0].s5()
    finish2()
    back = send
    go_back, done_back = a2a_copies(back, ret, bs, br, dp, mp, D)

    def ln_back(i, carry):
        r = rows(i * 64, 64)
        unit, inv = layer_norm(stream[r, :])
        dn = dnp[rows(mp * RD + i * 64, 64), :].astype(F32)
        e = (dn + fl2[r, :].astype(F32) + fr2[r, :].astype(F32)) * gain[...].astype(F32)
        dst = cotg[rows(mp * RD + i * 64, 64), :].astype(F32) + inv * (
            e
            - jnp.mean(e, axis=-1, keepdims=True)
            - unit * jnp.mean(e * unit, axis=-1, keepdims=True)
        )
        stream[r, :] = dst.astype(BF)
        return carry

    lax.fori_loop(0, RD // 64, ln_back, 0)

    def spread(i, carry):
        r = rows(i * 128, 128)
        code = idx[r, :].astype(F32)
        want = (lax.broadcasted_iota(jnp.int32, (128, 128), 1) + 1).astype(F32)
        lo = jnp.where(code == want, 1.0, 0.0).astype(BF)
        hi = jnp.where(code == want + 128.0, 1.0, 0.0).astype(BF)
        back[r, 0:D] = (mm(lo, stream[0:128, :]) + mm(hi, stream[128:256, :])).astype(BF)
        return carry

    lax.fori_loop(0, SLOTS // 128, spread, 0)
    go_back()
    st[3].s3()
    st[2].s4()
    st[1].s5()
    st[0].s6()
    st[3].s4()
    st[2].s5()
    st[1].s6()
    st[3].s5()
    st[2].s6()
    done_back()

    def collect(i, carry):
        r = rows(i * 128, 128)
        col = pl.ds(pl.multiple_of(i * 128, 128), 128)
        recv[r, 0:D] = mm(sel[:, col], ret[...], 0, 0).astype(BF)
        return carry

    lax.fori_loop(0, RD // 128, collect, 0)
    l_dp = pltpu.make_async_copy(recv.at[0:RD, 0:D], dpatch, ls.at[9])
    l_dp.start()
    st[3].s6()

    def settle(h, carry):
        Stage(h).s7()
        return carry

    lax.fori_loop(0, NH, settle, 0)
    c_drain()
    n_drain()
    drain()
    drain2()
    l_out.wait()
    l_dp.wait()


def sds(*shape):
    return jax.ShapeDtypeStruct(shape, BF)


def vm(*shape):
    return pltpu.VMEM(shape, BF)


def dma(*n):
    return pltpu.SemaphoreType.DMA(n)


def local(
    patch_rows, packing, segment, coords, pos_rows, pos_cols, norm_gain, w_qkv, w_out, cotangent
):
    h = RD // 2
    anywhere = pl.BlockSpec(memory_space=pl.ANY)
    output, d_patches, total = pl.pallas_call(
        sublayer_kernel,
        out_shape=(sds(RD, D), sds(RD, D), sds(4, NH * HP, D)),
        in_specs=[VM] * 6 + [anywhere] * 4,
        out_specs=[anywhere] * 3,
        scratch_shapes=[
            vm(RD, D), vm(SEQ, D), vm(SEQ, D), vm(SEQ, NH * 3 * HP), vm(SEQ, NH * HP),
            vm(SLOTS, 128), vm(SLOTS, RD), vm(NH * 3 * HP, D), vm(NH * HP, D),
            pltpu.VMEM((RD, 2), jnp.int32), pltpu.VMEM((SEQ, 1), jnp.int32),
            vm(SLOTS, D + 128), vm(SLOTS, D + 128), vm(SLOTS, D),
            vm(NH, 256, 2048), vm(SEQ, NH * HP),
            pltpu.VMEM((SEQ, HP), F32), pltpu.VMEM((SEQ, HP), F32),
            vm(SEQ, D), vm(SEQ, D), vm(4, NH * HP, D),
            vm(h, D), vm(h, D), vm(RD, D), vm(RD, D),
            vm(h, D), vm(h, D), vm(RD, D), vm(RD, D),
            vm(NH, 2, HP, D),
            vm(NH, 3, 64, CA), vm(NH, 3, 16, CA), vm(NH, 3, 64, D - CA), vm(NH, 3, 16, D - CA),
            dma(NDP), dma(NDP), dma(NDP), dma(NDP), dma(6), dma(6), dma(6), dma(6),
            dma(6), dma(6), dma(6), dma(6), dma(NH, 26), dma(NH, 26), dma(10), dma(NH, 2),
        ],
        compiler_params=pltpu.CompilerParams(
            collective_id=0, has_side_effects=True, vmem_limit_bytes=60 * 2**20
        ),
        name="sublayer",
    )(
        packing, coords, segment.reshape(1, SEQ), pos_rows, pos_cols,
        norm_gain.reshape(1, D), patch_rows, w_qkv.transpose(1, 2, 0), w_out, cotangent,
    )
    wide = total.reshape(4, NH, HP, D).astype(F32)
    grad_qkv = wide[:3, :, :HD].reshape(3, GW, D).transpose(2, 0, 1)
    grad_out = wide[3, :, :HD].reshape(GW, D)
    return (output, d_patches, grad_qkv, grad_out)


def solution(mesh):
    placed = (
        P(("dp", "mp"), None),
        P(None, ("dp", "mp")),
        P("dp"),
        P(None, ("dp", "mp")),
        P(),
        P(),
        P(),
        P(None, None, "mp"),
        P("mp", None),
        P(("dp", "mp"), None),
    )
    return jax.shard_map(
        local,
        mesh=mesh,
        in_specs=placed,
        out_specs=(
            P(("dp", "mp"), None),
            P(("dp", "mp"), None),
            P(None, None, "mp"),
            P("mp", None),
        ),
        check_vma=False,
    )
```

```python
import jax
import jax.numpy as jnp
from jax import lax
from jax.experimental import pallas as pl
from jax.experimental.pallas import tpu as pltpu
from jax.sharding import PartitionSpec as P

HD = 104
HP = 128
NH = 4
D = 1664
RD = 256
SEQ = 1024
CAP = 16
NDP = 32
SLOTS = NDP * CAP
CA = 896
GW = NH * HD
MESH = pl.DeviceIdType.MESH
F32 = jnp.float32
BF = jnp.bfloat16
VM = pl.BlockSpec(memory_space=pltpu.VMEM)
BLOCKS = ((0, 0, 256, 0), (256, 256, 768, 256), (512, 256, 1024, 768), (768, 512, 1024, 1536))


def mm(a, b, ca=1, cb=0):
    return lax.dot_general(a, b, (((ca,), (cb,)), ((), ())), preferred_element_type=F32)


def rows(start, size):
    return pl.ds(pl.multiple_of(start, 16), size)


def place():
    dp, mp = lax.axis_index("dp"), lax.axis_index("mp")
    return dp, mp, lax.rem(mp + 1, 4), lax.rem(mp + 3, 4), lax.rem(mp + 2, 4)


def copier(ssem, rsem):
    def make(src, dst, n, dev):
        return pltpu.make_async_remote_copy(
            src, dst, ssem.at[n], rsem.at[n], device_id=dev, device_id_type=MESH
        )

    return make


def greet(devs):
    bar = pltpu.get_barrier_semaphore()
    for dev in devs:
        pl.semaphore_signal(bar, inc=1, device_id=dev, device_id_type=MESH)
    return bar


def greet_dp(dp, mp, right, left):
    bar = greet(((dp, right), (dp, left)))

    def one(i, carry):
        pl.semaphore_signal(
            bar, inc=1, device_id=(lax.rem(dp + i, NDP), mp), device_id_type=MESH
        )
        return carry

    lax.fori_loop(1, NDP, one, 0)
    return bar


def a2a_copies(src, dst, ssem, rsem, dp, mp, first_col=0, width=D + 128, base=0):
    cols = pl.ds(first_col, width)

    def make(i):
        d = lax.rem(dp + i, NDP)
        return pltpu.make_async_remote_copy(
            src.at[rows(d * CAP, CAP), cols],
            dst.at[rows(dp * CAP, CAP), cols],
            ssem.at[base + i],
            rsem.at[base + i],
            device_id=(d, mp),
            device_id_type=MESH,
        )

    def start():
        def one(i, carry):
            make(i).start()
            return carry

        lax.fori_loop(1, NDP, one, 0)
        dst[rows(dp * CAP, CAP), cols] = src[rows(dp * CAP, CAP), cols]

    def wait():
        def one(i, carry):
            make(i).wait()
            return carry

        lax.fori_loop(1, NDP, one, 0)

    return start, wait


def ring_gather(src, dst, ssem, rsem, dp, mp, right, left, first_col=0, width=D, base=0):
    plain = copier(ssem, rsem)
    cols = pl.ds(first_col, width)
    h = RD // 2

    def make(a, b, n, dev):
        return plain(a, b, base + n, dev)

    def at(dev, half):
        return dst.at[rows(dev * RD + half * h, h), cols]

    a0 = make(src.at[0:h, cols], at(mp, 0), 0, (dp, right))
    b1 = make(src.at[h:RD, cols], at(mp, 1), 1, (dp, left))
    a1 = make(src.at[h:RD, cols], at(mp, 1), 2, (dp, right))
    b0 = make(src.at[0:h, cols], at(mp, 0), 3, (dp, left))
    f0 = make(at(left, 0), at(left, 0), 4, (dp, right))
    f1 = make(at(right, 1), at(right, 1), 5, (dp, left))

    def start():
        for c in (a0, b1, a1, b0):
            c.start()

    def onward():
        a0.wait_recv()
        f0.start()
        b1.wait_recv()
        f1.start()

    def near():
        a1.wait_recv()
        b0.wait_recv()

    def far():
        f0.wait_recv()
        f1.wait_recv()

    def drain():
        for c in (a0, b1, a1, b0, f0, f1):
            c.wait_send()

    return start, onward, near, far, drain


def ring_reduce(part, ha, hb, fl, fr, ssem, rsem, dp, mp, right, left, opp, first_col=0, width=D, base=0):
    plain = copier(ssem, rsem)
    cols = pl.ds(first_col, width)

    def make(src, dst, n, dev):
        return plain(src, dst, base + n, dev)

    h = RD // 2

    def at(dev, half):
        return part.at[rows(dev * RD + half * h, h), cols]

    s0 = make(at(opp, 0), ha.at[:, cols], 0, (dp, right))
    s1 = make(at(opp, 1), hb.at[:, cols], 1, (dp, left))
    s2 = make(at(right, 1), fl.at[h:RD, cols], 2, (dp, right))
    s3 = make(at(left, 0), fr.at[0:h, cols], 3, (dp, left))
    s4 = make(at(right, 0), fl.at[0:h, cols], 4, (dp, right))
    s5 = make(at(left, 1), fr.at[h:RD, cols], 5, (dp, left))

    def first():
        s0.start()
        s1.start()

    def second():
        s2.start()
        s3.start()

    def onward():
        s0.wait_recv()
        r0 = rows(right * RD, h)
        part[r0, cols] = (part[r0, cols].astype(F32) + ha[:, cols].astype(F32)).astype(BF)
        s4.start()
        s1.wait_recv()
        r1 = rows(left * RD + h, h)
        part[r1, cols] = (part[r1, cols].astype(F32) + hb[:, cols].astype(F32)).astype(BF)
        s5.start()

    def finish():
        for c in (s2, s3, s4, s5):
            c.wait_recv()

    def drain():
        for c in (s0, s1, s2, s3, s4, s5):
            c.wait_send()

    return first, second, onward, finish, drain


def column(row):
    n = row.shape[1]
    eye = lax.broadcasted_iota(jnp.int32, (n, n), 0) == lax.broadcasted_iota(jnp.int32, (n, n), 1)
    return jnp.sum(jnp.where(eye, row.astype(F32), 0.0), axis=1, keepdims=True).astype(jnp.int32)


def layer_norm(stream_rows):
    sf = stream_rows.astype(F32)
    cen = sf - jnp.mean(sf, axis=-1, keepdims=True)
    inv = lax.rsqrt(jnp.mean(cen * cen, axis=-1, keepdims=True) + 1e-06)
    return cen * inv, inv


def head_cols(h):
    return [pl.ds(pl.multiple_of(k * NH * HP + h * HP, 128), HP) for k in range(3)]


def sublayer_kernel(
    packing, coords, seg, prow, pcol, gain, patch_in, w_in, wo_in, cot_in,
    out, dpatch, total,
    stream, ng, cotg, qkv, datt, idx, sel, wq, wo, crd,
    send, recv, ret, prob, att, dk, part, dnp, grad,
    ha, hb, fl, fr, ha2, hb2, fl2, fr2, core_in, ax, az, bx, bz, stats,
    as_, ar, bs, br, cs, cr, ns, nr, os_, or_, ys, yr, gs, gr, ls, lk,
):
    dp, mp, right, left, opp = place()
    c = lax.rem(dp, 2)
    x = lax.rem(dp // 2, 4)
    z = dp // 8
    other = 1 - c
    scale = HD ** (-0.5)
    coef = (RD * NDP * 4) ** (-0.5)
    bar = greet_dp(dp, mp, right, left)
    l_w = pltpu.make_async_copy(w_in, grad.at[0:3, 0:GW], ls.at[0])
    l_o = pltpu.make_async_copy(wo_in, grad.at[3, 0:GW], ls.at[1])
    l_c = pltpu.make_async_copy(cot_in, cotg.at[rows(mp * RD, RD)], ls.at[2])
    patch = part.at[0:RD]
    l_p = pltpu.make_async_copy(patch_in, patch, ls.at[7])
    l_p.start()
    l_c.start()
    l_w.start()
    l_o.start()

    g_row = packing[0:1, :]
    src_i = lax.broadcasted_iota(jnp.int32, (RD, RD), 0)
    dst_i = lax.broadcasted_iota(jnp.int32, (RD, RD), 1)
    before = jnp.where((column(g_row) == g_row) & (src_i < dst_i), 1.0, 0.0)
    rank = jnp.sum(before, axis=0, keepdims=True).astype(jnp.int32)
    placed = g_row * CAP + rank
    ext = jnp.broadcast_to((column(packing[1:2, :]) + 1).astype(F32), (RD, 128)).astype(BF)

    l_p.wait()

    def fill(i, carry):
        at = rows(i * 128, 128)
        slot = lax.broadcasted_iota(jnp.int32, (128, RD), 0) + i * 128
        pick = jnp.where(slot == placed, 1.0, 0.0).astype(BF)
        sel[at, :] = pick
        send[at, 0:D] = mm(pick, patch[...]).astype(BF)
        send[at, D:] = mm(pick, ext).astype(BF)
        return carry

    l_c.wait()
    cot_own = cotg.at[rows(mp * RD, RD)]
    cg = [
        ring_gather(cot_own, cotg, cs, cr, dp, mp, right, left, first_col, width, base)
        for first_col, width, base in ((0, D - CA, 0), (D - CA, CA, 6))
    ]
    pl.semaphore_wait(bar, NDP + 1)
    cg[0][0]()
    lax.fori_loop(0, SLOTS // 128, fill, 0)
    a2a = [
        a2a_copies(send, recv, as_, ar, dp, mp, first_col, width, base)
        for first_col, width, base in ((CA, D + 128 - CA, 0), (0, CA, NDP))
    ]
    a2a[0][0]()
    a2a[1][0]()

    crd[:, 0:1] = column(coords[0:1, :])
    crd[:, 1:2] = column(coords[1:2, :])
    for i in range(4):
        crd[:, 2 + i : 3 + i] = column(seg[:, i * 256 : (i + 1) * 256])
    l_w.wait()
    l_o.wait()

    def pad_head(h, carry):
        i0 = lax.broadcasted_iota(jnp.int32, (HP, GW), 0)
        i1 = lax.broadcasted_iota(jnp.int32, (HP, GW), 1)
        pick = jnp.where((i1 == i0 + h * HD) & (i0 < HD), 1.0, 0.0).astype(BF)

        def one(k, inner):
            wq[rows(k * NH * HP + h * HP, HP), :] = mm(pick, grad[k, 0:GW, :]).astype(BF)
            return inner

        lax.fori_loop(0, 3, one, 0)
        wo[rows(h * HP, HP), :] = mm(pick, grad[3, 0:GW, :]).astype(BF)
        return carry

    lax.fori_loop(0, NH, pad_head, 0)
    cg[0][1]()
    a2a[0][1]()
    idx[...] = recv[:, D:]

    def unpack(first_col, width):
        cols = pl.ds(first_col, width)

        def one(i, carry):
            at = rows(i * 128, 128)
            code = recv[:, D:].astype(F32)
            want = (lax.broadcasted_iota(jnp.int32, (SLOTS, 128), 1) + (i * 128 + 1)).astype(F32)
            pick = jnp.where(code == want, 1.0, 0.0).astype(BF)
            packed = mm(pick, recv[:, cols], 0, 0)
            gi = lax.broadcasted_iota(jnp.int32, (128, 16), 1)
            row_hot = jnp.where(gi == crd[at, 0:1], 1.0, 0.0).astype(BF)
            col_hot = jnp.where(gi == crd[at, 1:2], 1.0, 0.0).astype(BF)
            pos = mm(row_hot, prow[:, cols]) + mm(col_hot, pcol[:, cols])
            stream[at, cols] = (packed + pos).astype(BF)
            return carry

        lax.fori_loop(0, RD // 128, one, 0)

    sg = [
        ring_gather(stream, dnp, ns, nr, dp, mp, right, left, first_col, width, base)
        for first_col, width, base in ((CA, D - CA, 0), (0, CA, 6))
    ]
    unpack(CA, D - CA)
    sg[0][0]()
    sg[0][1]()
    a2a[1][1]()
    unpack(0, CA)
    sg[1][0]()

    def normalize(s, src, first_row):
        def one(i, carry):
            unit, _ = layer_norm(src[rows(first_row + i * 64, 64), 0:D])
            ng[rows(s * RD + i * 64, 64), :] = (unit * gain[...].astype(F32)).astype(BF)
            return carry

        lax.fori_loop(0, RD // 64, one, 0)

    def project(s):
        def one(n, carry):
            col = pl.ds(pl.multiple_of(n * 512, 128), 512)
            qkv[rows(s * RD, RD), col] = mm(
                ng[rows(s * RD, RD)], wq[rows(n * 512, 512), :], 1, 1
            ).astype(BF)
            return carry

        lax.fori_loop(0, 3, one, 0)

    def back_project(s):
        datt[rows(s * RD, RD), :] = mm(cotg[rows(s * RD, RD)], wo[...], 1, 1).astype(BF)

    normalize(mp, stream, 0)
    project(mp)
    sg[1][1]()
    cg[1][0]()
    sg[0][2]()
    sg[1][2]()
    for s in (right, left):
        normalize(s, dnp, s * RD)
        project(s)
    sg[0][3]()
    sg[1][3]()
    normalize(opp, dnp, opp * RD)
    project(opp)

    def fwd(h, carry):
        qc, kc, vc = head_cols(h)
        hc = pl.ds(pl.multiple_of(h * HP, 128), HP)
        for r0, k0, k1, p0 in BLOCKS:
            s = mm(qkv[r0 : r0 + 256, qc], qkv[k0:k1, kc], 1, 1) * scale
            same = crd[:, 2 + r0 // 256 : 3 + r0 // 256] == seg[:, k0:k1]
            s = jnp.where(same, s, -1e30)
            e = jnp.where(same, jnp.exp(s - jnp.max(s, axis=-1, keepdims=True)), 0.0)
            p = (e / jnp.sum(e, axis=-1, keepdims=True)).astype(BF)
            prob[h, :, p0 : p0 + k1 - k0] = p
            att[r0 : r0 + 256, hc] = mm(p, qkv[k0:k1, vc]).astype(BF)

        @pl.when(h == 1)
        def _():
            cg[1][1]()

        return carry

    lax.fori_loop(0, NH, fwd, 0)
    first, second, onward, finish, drain = ring_reduce(
        part, ha, hb, fl, fr, os_, or_, dp, mp, right, left, opp
    )

    def out_rows(s):
        part[rows(s * RD, RD), :] = mm(att[rows(s * RD, RD), :], wo[...]).astype(BF)

    out_rows(opp)
    first()
    out_rows(right)
    out_rows(left)
    second()
    out_rows(mp)
    for k in range(2):
        cg[k][2]()
        cg[k][3]()
    for s in (mp, right, left, opp):
        back_project(s)

    def dev(zz, xx, cc):
        return ((zz * 4 + xx) * 2 + cc, mp)

    def shift(v, s):
        return lax.rem(v + s, 4)

    halves = (pl.ds(0, CA), pl.ds(CA, D - CA))

    def piece(k, r, size, cols):
        return grad.at[k, rows(c * RD + r, size), cols]

    def placed_piece(k, r, size, cols):
        return total.at[k, rows(c * RD + r, size), cols]

    class Stage:
        def __init__(self, h):
            def make(src, dst, n, to):
                return pltpu.make_async_remote_copy(
                    src, dst, gs.at[h, n], gr.at[h, n], device_id=to, device_id_type=MESH
                )

            def far(axis, s):
                return dev(z, shift(x, s), c) if axis == 0 else dev(shift(z, s), x, c)

            self.h = h
            self.make, self.far = make, far

        def swap(self):
            return self.make(
                grad.at[self.h, rows(other * RD, RD)], core_in.at[self.h], 0, dev(z, x, other)
            )

        def last(self):
            ours = total.at[self.h, rows(c * RD, RD)]
            return self.make(ours, ours, 25, dev(z, x, other))

        def group(self, kind, a):
            one, two = (x, z) if a == 0 else (z, x)
            copies = []
            for s in (1, 2, 3):
                if kind == 0:
                    src = piece(self.h, shift(one, s) * 64, 64, halves[a])
                    dst = (ax, bx)[a].at[self.h, s - 1]
                elif kind == 1:
                    src = piece(self.h, one * 64 + shift(two, s) * 16, 16, halves[a])
                    dst = (az, bz)[a].at[self.h, s - 1]
                elif kind == 2:
                    src = piece(self.h, one * 64 + two * 16, 16, halves[a])
                    dst = placed_piece(self.h, one * 64 + two * 16, 16, halves[a])
                else:
                    src = dst = placed_piece(self.h, one * 64, 64, halves[a])
                axis = a if kind in (0, 3) else 1 - a
                copies.append(self.make(src, dst, 12 * a + 3 * kind + s, self.far(axis, s)))
            return copies

        def keep(self, a):
            one, two = (x, z) if a == 0 else (z, x)
            r = one * 64 + two * 16
            return pltpu.make_async_copy(
                piece(self.h, r, 16, halves[a]),
                placed_piece(self.h, r, 16, halves[a]),
                lk.at[self.h, a],
            )

        def s0(self):
            self.swap().start()

        def s1(self):
            h = self.h
            self.swap().wait_recv()
            for i in range(2):
                r, q = rows(c * RD + i * 128, 128), slice(i * 128, (i + 1) * 128)
                grad[h, r, :] = (grad[h, r, :].astype(F32) + core_in[h, q].astype(F32)).astype(BF)
            big = self.group(0, 0), self.group(0, 1)
            for s in (1, 0, 2):
                for a in range(2):
                    big[a][s].start()

        def gather(self, copies, ref, incoming, nxt):
            for q in copies:
                q.wait_recv()
            val = ref[...].astype(F32)
            for s in range(3):
                val += incoming[self.h, s].astype(F32)
            ref[...] = val.astype(BF)
            for q in nxt:
                q.start()

        def s2(self):
            for a, b_in in enumerate((ax, bx)):
                one = x if a == 0 else z
                ref = piece(self.h, one * 64, 64, halves[a])
                self.gather(self.group(0, a), ref, b_in, self.group(1, a))

        def s3(self):
            for a, s_in in enumerate((az, bz)):
                one, two = (x, z) if a == 0 else (z, x)
                ref = piece(self.h, one * 64 + two * 16, 16, halves[a])
                self.gather(self.group(1, a), ref, s_in, self.group(2, a) + [self.keep(a)])

        def s4(self):
            for a in range(2):
                self.keep(a).wait()
                for q in self.group(2, a):
                    q.wait_recv()
                for q in self.group(3, a):
                    q.start()

        def s5(self):
            for a in range(2):
                for q in self.group(3, a):
                    q.wait_recv()
            self.last().start()

        def s6(self):
            self.last().wait_recv()

        def s7(self):
            sent = [self.swap(), self.last()]
            for kind in range(4):
                sent += self.group(kind, 0) + self.group(kind, 1)
            for q in sent:
                q.wait_send()

    st = [Stage(k) for k in range(4)]
    grad[3] = (mm(att[...], cotg[...], 0, 0) * coef).astype(BF)
    st[3].s0()

    def bwd_value(h, carry):
        hc = pl.ds(pl.multiple_of(h * HP, 128), HP)
        hc2 = pl.ds(pl.multiple_of(NH * HP + h * HP, 128), HP)
        dk[...] = jnp.zeros_like(dk)
        for r0, k0, k1, p0 in BLOCKS:
            dk[k0:k1, :] += mm(prob[h, :, p0 : p0 + k1 - k0], datt[r0 : r0 + 256, hc], 0, 0)
        recv[:, hc] = dk[0:512, :].astype(BF)
        recv[:, hc2] = dk[512:SEQ, :].astype(BF)
        return carry

    lax.fori_loop(0, NH, bwd_value, 0)
    d_value = mm(recv[:, 0:512], ng[0:512], 0, 0) + mm(recv[:, 512:1024], ng[512:SEQ], 0, 0)
    grad[2] = (d_value * coef).astype(BF)
    st[2].s0()
    st[3].s1()

    def bwd(h, carry):
        qc, kc, vc = head_cols(h)
        hc = pl.ds(pl.multiple_of(h * HP, 128), HP)
        dk[...] = jnp.zeros_like(dk)
        for r0, k0, k1, p0 in BLOCKS:
            p = prob[h, :, p0 : p0 + k1 - k0]
            da = datt[r0 : r0 + 256, hc]
            delta = jnp.sum(
                da.astype(F32) * att[r0 : r0 + 256, hc].astype(F32), axis=-1, keepdims=True
            )
            dprob = mm(da, qkv[k0:k1, vc], 1, 1)
            ds = (p.astype(F32) * (dprob - delta) * scale).astype(BF)
            dk[k0:k1, :] += mm(ds, qkv[r0 : r0 + 256, qc], 0, 0)
            qkv[r0 : r0 + 256, qc] = mm(ds, qkv[k0:k1, kc]).astype(BF)
        qkv[:, kc] = dk[...].astype(BF)
        hc2 = pl.ds(pl.multiple_of(NH * HP + h * HP, 128), HP)
        qkv[0:512, vc] = recv[:, hc]
        qkv[512:SEQ, vc] = recv[:, hc2]

        @pl.when(h == 0)
        def _():
            st[2].s1()

        @pl.when(h == 1)
        def _():
            onward()
            st[3].s2()

        @pl.when(h == 2)
        def _():
            st[2].s2()
            st[3].s3()

        @pl.when(h == 3)
        def _():
            st[3].s4()
            st[2].s3()

        return carry

    lax.fori_loop(0, NH, bwd, 0)

    def weight_grad(k):
        cols = pl.ds(k * NH * HP, NH * HP)
        grad[k] = (mm(qkv[:, cols], ng[...], 0, 0) * coef).astype(BF)
        st[k].s0()

    sg[0][4]()
    sg[1][4]()
    rs = [
        ring_reduce(
            dnp, ha2, hb2, fl2, fr2, ys, yr, dp, mp, right, left, opp, first_col, width, base
        )
        for first_col, width, base in ((0, HP + CA, 0), (HP + CA, D - CA, 6))
    ]

    def d_rows(s):
        def one(i, carry):
            r = rows(s * RD + i * 128, 128)
            v = mm(qkv[r, :], wq[...])
            dnp[r, HP:] = v.astype(BF)
            m1 = jnp.sum(v * gain[...].astype(F32), axis=-1, keepdims=True) * (1.0 / D)
            m2 = jnp.sum(v * ng[r, :].astype(F32), axis=-1, keepdims=True) * (1.0 / D)
            lane = lax.broadcasted_iota(jnp.int32, (128, HP), 1)
            dnp[r, 0:HP] = jnp.where(lane < HP // 2, m1, m2).astype(BF)
            return carry

        lax.fori_loop(0, 2, one, 0)

    d_rows(opp)
    rs[0][0]()
    d_rows(right)
    d_rows(left)
    rs[0][1]()
    rs[1][0]()
    rs[1][1]()
    weight_grad(0)
    weight_grad(1)
    d_rows(mp)
    st[2].s4()
    st[3].s5()
    rs[0][2]()
    st[0].s1()
    st[1].s1()
    rs[1][2]()
    finish()
    acc = part[rows(mp * RD, RD)].astype(F32) + fl[...].astype(F32) + fr[...].astype(F32)
    part[rows(mp * RD, RD)] = (stream[...].astype(F32) + acc).astype(BF)
    l_out = pltpu.make_async_copy(part.at[rows(mp * RD, RD)], out, ls.at[8])
    l_out.start()
    st[2].s5()
    back = send

    def ln_stats(i, carry):
        r = rows(i * 64, 64)
        sf = stream[r, :].astype(F32)
        mean = jnp.mean(sf, axis=-1, keepdims=True)
        cen = sf - mean
        stats[r, 0:1] = mean
        stats[r, 1:2] = lax.rsqrt(jnp.mean(cen * cen, axis=-1, keepdims=True) + 1e-06)
        return carry

    lax.fori_loop(0, RD // 64, ln_stats, 0)

    def total_of(i, cols):
        r = rows(i * 64, 64)
        own = dnp[rows(mp * RD + i * 64, 64), cols].astype(F32)
        return own + fl2[r, cols].astype(F32) + fr2[r, cols].astype(F32)

    def chunk(first_col, width):
        here, there = pl.ds(first_col, width), pl.ds(HP + first_col, width)

        def ln_back(i, carry):
            r = rows(i * 64, 64)
            if first_col == 0:
                both = total_of(i, pl.ds(0, HP))
                stats[r, 2:3] = both[:, 0:1]
                stats[r, 3:4] = both[:, HP // 2 : HP // 2 + 1]
            inv = stats[r, 1:2]
            unit = (stream[r, here].astype(F32) - stats[r, 0:1]) * inv
            e = total_of(i, there) * gain[:, here].astype(F32)
            dst = cotg[rows(mp * RD + i * 64, 64), here].astype(F32) + inv * (
                e - stats[r, 2:3] - unit * stats[r, 3:4]
            )
            stream[r, here] = dst.astype(BF)
            return carry

        lax.fori_loop(0, RD // 64, ln_back, 0)

        def spread(i, carry):
            r = rows(i * 128, 128)
            code = idx[r, :].astype(F32)
            want = (lax.broadcasted_iota(jnp.int32, (128, 128), 1) + 1).astype(F32)
            lo = jnp.where(code == want, 1.0, 0.0).astype(BF)
            hi = jnp.where(code == want + 128.0, 1.0, 0.0).astype(BF)
            back[r, here] = (mm(lo, stream[0:128, here]) + mm(hi, stream[128:256, here])).astype(BF)
            return carry

        lax.fori_loop(0, SLOTS // 128, spread, 0)

    backs = [
        a2a_copies(back, ret, bs, br, dp, mp, first_col, width, base)
        for first_col, width, base in ((0, CA, 0), (CA, D - CA, NDP))
    ]
    st[0].s2()
    st[1].s2()
    rs[0][3]()
    chunk(0, CA)
    backs[0][0]()
    st[3].s6()
    st[0].s3()
    st[1].s3()
    rs[1][3]()
    chunk(CA, D - CA)
    backs[1][0]()
    st[2].s6()
    st[0].s4()
    st[1].s4()
    st[0].s5()
    st[1].s5()
    backs[0][1]()
    backs[1][1]()

    def collect(i, carry):
        r = rows(i * 128, 128)
        col = pl.ds(pl.multiple_of(i * 128, 128), 128)
        recv[r, 0:D] = mm(sel[:, col], ret[...], 0, 0).astype(BF)
        return carry

    lax.fori_loop(0, RD // 128, collect, 0)
    l_dp = pltpu.make_async_copy(recv.at[0:RD, 0:D], dpatch, ls.at[9])
    l_dp.start()
    st[0].s6()
    st[1].s6()

    def settle(h, carry):
        Stage(h).s7()
        return carry

    lax.fori_loop(0, NH, settle, 0)
    cg[0][4]()
    cg[1][4]()
    drain()
    rs[0][4]()
    rs[1][4]()
    l_out.wait()
    l_dp.wait()


def sds(*shape):
    return jax.ShapeDtypeStruct(shape, BF)


def vm(*shape):
    return pltpu.VMEM(shape, BF)


def dma(*n):
    return pltpu.SemaphoreType.DMA(n)


def local(
    patch_rows, packing, segment, coords, pos_rows, pos_cols, norm_gain, w_qkv, w_out, cotangent
):
    h = RD // 2
    anywhere = pl.BlockSpec(memory_space=pl.ANY)
    output, d_patches, total = pl.pallas_call(
        sublayer_kernel,
        out_shape=(sds(RD, D), sds(RD, D), sds(4, NH * HP, D)),
        in_specs=[VM] * 6 + [anywhere] * 4,
        out_specs=[anywhere] * 3,
        scratch_shapes=[
            vm(RD, D), vm(SEQ, D), vm(SEQ, D), vm(SEQ, NH * 3 * HP), vm(SEQ, NH * HP),
            vm(SLOTS, 128), vm(SLOTS, RD), vm(NH * 3 * HP, D), vm(NH * HP, D),
            pltpu.VMEM((RD, 6), jnp.int32),
            vm(SLOTS, D + 128), vm(SLOTS, D + 128), vm(SLOTS, D),
            vm(NH, 256, 2048), vm(SEQ, NH * HP),
            pltpu.VMEM((SEQ, HP), F32),
            vm(SEQ, D), vm(SEQ, D + HP), vm(4, NH * HP, D),
            vm(h, D), vm(h, D), vm(RD, D), vm(RD, D),
            vm(h, D + HP), vm(h, D + HP), vm(RD, D + HP), vm(RD, D + HP),
            vm(NH, RD, D),
            vm(NH, 3, 64, CA), vm(NH, 3, 16, CA), vm(NH, 3, 64, D - CA), vm(NH, 3, 16, D - CA),
            pltpu.VMEM((RD, 4), F32),
            dma(2 * NDP), dma(2 * NDP), dma(2 * NDP), dma(2 * NDP),
            dma(12), dma(12), dma(12), dma(12),
            dma(6), dma(6), dma(12), dma(12), dma(NH, 26), dma(NH, 26), dma(10), dma(NH, 2),
        ],
        compiler_params=pltpu.CompilerParams(
            collective_id=0, has_side_effects=True, vmem_limit_bytes=60 * 2**20
        ),
        name="sublayer",
    )(
        packing, coords, segment.reshape(1, SEQ), pos_rows, pos_cols,
        norm_gain.reshape(1, D), patch_rows, w_qkv.transpose(1, 2, 0), w_out, cotangent,
    )
    wide = total.reshape(4, NH, HP, D).astype(F32)
    grad_qkv = wide[:3, :, :HD].reshape(3, GW, D).transpose(2, 0, 1)
    grad_out = wide[3, :, :HD].reshape(GW, D)
    return (output, d_patches, grad_qkv, grad_out)


def solution(mesh):
    placed = (
        P(("dp", "mp"), None),
        P(None, ("dp", "mp")),
        P("dp"),
        P(None, ("dp", "mp")),
        P(),
        P(),
        P(),
        P(None, None, "mp"),
        P("mp", None),
        P(("dp", "mp"), None),
    )
    return jax.shard_map(
        local,
        mesh=mesh,
        in_specs=placed,
        out_specs=(
            P(("dp", "mp"), None),
            P(("dp", "mp"), None),
            P(None, None, "mp"),
            P("mp", None),
        ),
        check_vma=False,
    )
```
